512 devices in a mesh: expert: 16 (over z), tensor: 32 (over y, x, core).
Axes of the slice: x: 4, y: 4, z: 16, core: 2. Of those that a mesh axis runs over, the one named last changes fastest.
Arguments:
- tokens: bfloat16 [512, 3072], P('expert', 'tensor'), may hold values from -6 to 6
- routes: int32 [512, 4], P('expert'), may hold values from 0 to 15, all different within a row; in each aligned block of 32 rows (0 to 31, 32 to 63, ...) at most 16 rows name the same one
- route_weight: int32 [512, 4], P('expert'), may hold values from 1 to 255
- w_gate: bfloat16 [16, 5376, 3072], P('expert', 'tensor'), may hold values from -0.109375 to 0.109375
- w_up: bfloat16 [16, 5376, 3072], P('expert', 'tensor'), may hold values from -0.109375 to 0.109375
- w_down: bfloat16 [16, 5376, 3072], P('expert', 'tensor'), may hold values from -0.078125 to 0.078125
Outputs:
- mixed: bfloat16 [512, 3072], P('expert', 'tensor')
The draws below stay inside these ranges and needn't reach their ends.
Inputs may be any that keep to these rules, and one draw needn't show every extreme that they name: `routes`: within each aligned block of 32 rows the 4 experts of a row differ, no expert is named by more than 16 rows, a bound that some block reaches.
All inputs are finite; a program needn't handle non-finite values.
Results may differ from the reference program's by a relative error of at most 0.02.
Values may be sent and summed in bfloat16 or wider, within the bound.
No kernel may reach another device: no remote copies, remote signals or barrier semaphores. Data moves between devices by JAX's collectives and lax.ppermute only.
A program may use at most 64 MiB of HBM per device.

```python
import math
import jax
import jax.numpy as jnp
import numpy as np
from jax import lax

D = 3072
FF = 5376
TOP = 4
ROWS_DEV = 32
EXPERTS = 16
BATCH = 512
CAP = 16
N_TENSOR = 32


def set_ends(drawn, key, low, high):
    longest = drawn.shape.index(max(drawn.shape))
    spots = []
    for shift in (0, 1):
        where = [jax.random.randint(jax.random.fold_in(key, axis), (), 0, length) for axis, length in enumerate(drawn.shape)]
        where[longest] = (where[longest] + shift) % drawn.shape[longest]
        spots.append(tuple(where))
    return drawn.at[spots[0]].set(low).at[spots[1]].set(high)


def levels(key, shape, pieces, smallest, largest):
    def one(dim, blocks):
        steps = jax.random.uniform(jax.random.fold_in(jax.random.fold_in(key, 6), dim), (blocks,), jnp.float32, smallest / len(pieces), largest / len(pieces))
        return jnp.repeat(jnp.exp(steps), shape[dim] // blocks).reshape((-1,) + (1,) * (len(shape) - dim - 1))

    gain = one(*pieces[0])
    for cut in pieces[1:]:
        gain = gain * one(*cut)
    return gain


def deal_out(stream_key, own, number, rows, number_of, top, most, slope):
    order = jax.random.permutation(stream_key, number_of)
    packed, common = load_shares(number_of, rows * top, most, slope, True), load_shares(number_of, rows * top, most, slope, False)
    places = jnp.arange(number_of)

    def named(tallies, rotation):
        used = int((tallies > 0).sum())
        fixed = max(1, used // 4)
        shifted = fixed + (places - fixed + rotation * (used - fixed)) % max(1, number_of - fixed)
        return jnp.zeros((number_of,), jnp.int32).at[order[jnp.where(places < fixed, places, shifted)]].set(jnp.asarray(tallies, jnp.int32))

    tallies = jnp.where(number % 4 == 0, named(packed, number // 4), named(common, number - number // 4 - 1))
    mixed = jax.random.permutation(jax.random.fold_in(own, 3), number_of)
    donor, sink = mixed[0:number_of // 2 * 2:2], mixed[1:number_of // 2 * 2:2]
    room = jnp.minimum(tallies[donor] - 1, most - tallies[sink]) // 2
    room = jnp.where((donor == order[0]) | (sink == order[0]) | (tallies[sink] == 0), 0, jnp.maximum(room, 0))
    shifted = jax.random.randint(jax.random.fold_in(own, 4), (number_of // 2,), 0, 1 << 20) % (room + 1)
    tallies = tallies.at[donor].add(-shifted).at[sink].add(shifted)
    labels = jnp.searchsorted(jnp.cumsum(tallies), jnp.arange(rows * top), side="right").astype(jnp.int32)
    grid = labels.reshape(top, rows).T
    grid = grid[jax.random.permutation(jax.random.fold_in(own, 1), rows)]
    rotation = jax.random.randint(jax.random.fold_in(own, 2), (rows, 1), 0, top)
    return jnp.take_along_axis(grid, (jnp.arange(top)[None, :] + rotation) % top, axis=1)


def load_shares(number_of, total, most, skew, full):
    loads = [(1 << 20) // math.isqrt(grade ** skew) + 1 for grade in range(1, number_of + 1)]
    largest = most if full else min(most, max(-(-total // number_of), total * loads[0] // sum(loads)))
    least = 1 if total - largest >= number_of - 1 else 0
    given, rest = [largest] + [least] * (number_of - 1), total - largest - least * (number_of - 1)
    while rest > 0:
        candidates = [i for i in range(1, number_of) if given[i] < largest] or [i for i in range(1, number_of) if given[i] < most]
        whole, budget = sum([loads[i] for i in candidates]), rest
        for i in candidates:
            addition = min(most - given[i], max(1, budget * loads[i] // whole), rest)
            given[i] = given[i] + addition
            rest = rest - addition
    return np.array(given)


def normal_values(own_key, shape, width, most, pieces=(), held_as=jnp.bfloat16):
    loudness = levels(own_key, shape, pieces, -0.22, 0.18) if pieces else 1.0
    array = jax.random.normal(own_key, shape, jnp.float32) * width * loudness
    return jnp.minimum(jnp.maximum(array, -most), most).astype(held_as)


def setup_inputs(seed: int = 0) -> dict:
    keys = jax.random.split(jax.random.key(seed), 7)
    tokens = normal_values(keys[0], (BATCH, D), 1.0, 6.0, ((0, 16), (1, 32)))
    routes_keys = jax.random.split(jax.random.fold_in(keys[1], 1), BATCH // ROWS_DEV)
    routes_turns = jax.random.permutation(jax.random.fold_in(keys[1], 3), BATCH // ROWS_DEV)
    routes = jax.vmap(lambda own, number: deal_out(jax.random.fold_in(keys[1], 2), own, number, ROWS_DEV, EXPERTS, TOP, CAP, 2))(routes_keys, routes_turns).reshape((BATCH, TOP))
    route_weight = set_ends(jax.random.randint(keys[2], (BATCH, TOP), 1, 256), jax.random.fold_in(keys[2], 1), 1, 255).astype(jnp.int32)
    w_gate = normal_values(keys[3], (EXPERTS, FF, D), D ** -0.5, 0.109375, ((0, 16), (1, 32)))
    w_up = normal_values(keys[4], (EXPERTS, FF, D), D ** -0.5, 0.109375, ((0, 16), (1, 32)))
    w_down = normal_values(keys[5], (EXPERTS, FF, D), FF ** -0.5, 0.078125, ((0, 16), (1, 32)))
    return {"tokens": tokens, "routes": routes, "route_weight": route_weight, "w_gate": w_gate, "w_up": w_up, "w_down": w_down}


def reference(tokens, routes, route_weight, w_gate, w_up, w_down):
    blocks = BATCH // ROWS_DEV
    flat = routes.reshape(blocks, ROWS_DEV * TOP)
    marks = (flat[:, :, None] == jnp.arange(EXPERTS, dtype=jnp.int32)[None, None, :]).astype(jnp.int32)
    before = jnp.cumsum(marks, axis=1) - marks
    slot = jnp.sum(before * marks, axis=2).astype(jnp.int32)
    source = jnp.broadcast_to(jnp.arange(blocks, dtype=jnp.int32)[:, None], flat.shape)
    row_index = jnp.repeat(jnp.arange(BATCH, dtype=jnp.int32), TOP).reshape(blocks, ROWS_DEV * TOP)
    buffer = jnp.zeros((EXPERTS, blocks, CAP, D), jnp.bfloat16)
    buffer = buffer.at[flat, source, slot].set(tokens[row_index])
    group = FF // N_TENSOR

    def expert_out(items):
        rows, gate_w, up_w, down_w = items
        rows = rows.reshape(blocks * CAP, D)
        gate = jnp.dot(rows, gate_w.T, preferred_element_type=jnp.float32)
        up = jnp.dot(rows, up_w.T, preferred_element_type=jnp.float32)
        hidden = (jax.nn.silu(gate) * up).astype(jnp.bfloat16)
        total = jnp.zeros((blocks * CAP, D), jnp.float32)
        for part_index in range(N_TENSOR):
            lower = part_index * group
            piece = jnp.dot(hidden[:, lower:lower + group], down_w[lower:lower + group], preferred_element_type=jnp.float32)
            piece = lax.optimization_barrier(piece.astype(jnp.bfloat16))
            total = total + piece.astype(jnp.float32)
        return total.reshape(blocks, CAP, D)

    outputs = lax.map(expert_out, (buffer, w_gate, w_up, w_down))
    picked = outputs[flat, source, slot].reshape(BATCH, TOP, D)
    weight_f = route_weight.astype(jnp.float32)
    share = weight_f / jnp.sum(weight_f, axis=1, keepdims=True)
    mixed = jnp.sum(picked * share[:, :, None], axis=1)
    return mixed.astype(jnp.bfloat16)
```

```python
import functools

import jax
import jax.numpy as jnp
from jax import lax
from jax.experimental import pallas as pl
from jax.experimental.pallas import tpu as pltpu
from jax.sharding import Mesh, PartitionSpec as P

GRID = ("y", "x")
VMEM = pl.BlockSpec(memory_space=pltpu.VMEM)
BF16 = jnp.bfloat16
F32 = jnp.float32


def dot(left, right, dims, precision=None):
    return lax.dot_general(left, right, (dims, ((), ())), precision=precision, preferred_element_type=F32)


def eye(n):
    same = lax.broadcasted_iota(jnp.int32, (n, n), 0) == lax.broadcasted_iota(jnp.int32, (n, n), 1)
    return same.astype(F32).astype(BF16)


def call(body, out, operands, scratch=(), flops=0, moved=0):
    return pl.pallas_call(
        body,
        out_shape=out,
        in_specs=[VMEM] * len(operands),
        out_specs=jax.tree.map(lambda _: VMEM, out),
        scratch_shapes=list(scratch),
        compiler_params=pltpu.CompilerParams(vmem_limit_bytes=40 * 2**20),
        cost_estimate=pl.CostEstimate(flops=flops, bytes_accessed=moved, transcendentals=0),
    )(*operands)


def place_kernel(capacity, tokens_ref, routes_ref, weight_ref, placed_ref, mix_ref):
    rows, top = routes_ref.shape
    columns = placed_ref.shape[0]
    column = lax.broadcasted_iota(jnp.int32, (rows, columns), 1)
    expert = column // capacity
    spot = column % capacity
    weight = weight_ref[...].astype(F32)
    share = weight / jnp.sum(weight, axis=1, keepdims=True)
    named = jnp.zeros((rows, columns), F32)
    mix = jnp.zeros((rows, columns), F32)
    for k in range(top):
        hit = routes_ref[:, k : k + 1] == expert
        named += jnp.where(hit, 1.0, 0.0)
        mix += jnp.where(hit, share[:, k : k + 1], 0.0)
    earlier = lax.broadcasted_iota(jnp.int32, (rows, rows), 1) < lax.broadcasted_iota(jnp.int32, (rows, rows), 0)
    before = dot(earlier.astype(F32).astype(BF16), named.astype(BF16), ((1,), (0,)))
    here = (named > 0.5) & (before.astype(jnp.int32) == spot)
    mix_ref[...] = jnp.where(here, mix, 0.0)
    dispatch = jnp.where(here, 1.0, 0.0).astype(BF16)
    placed_ref[...] = dot(dispatch, tokens_ref[...], ((0,), (0,))).astype(BF16)


def turn_kernel(arrived_ref, copies_ref):
    n, depth, _ = copies_ref.shape
    turned = dot(eye(depth), arrived_ref[...], ((1,), (1,))).astype(BF16)
    for i in range(n):
        copies_ref[i] = turned


def expert_kernel(own_ref, other_ref, core_ref, gate_ref, up_ref, down_ref, keep_ref, send_ref, x_ref, part_ref):
    n, depth, _ = own_ref.shape
    core = core_ref[0]

    def rows(i, which):
        return pl.ds(pl.multiple_of((2 * i + which) * depth, depth), depth)

    for i in range(n):
        x_ref[rows(i, core)] = own_ref[i]
        x_ref[rows(i, 1 - core)] = other_ref[i]
    gate = dot(gate_ref[...], x_ref[...], ((1,), (0,)))
    up = dot(up_ref[...], x_ref[...], ((1,), (0,)))
    hidden = (gate / (1.0 + jnp.exp(-gate)) * up).astype(BF16)
    part_ref[...] = dot(down_ref[...], hidden, ((0,), (0,))).astype(BF16)
    for i in range(n):
        keep_ref[i] = part_ref[rows(i, core)]
        send_ref[i] = part_ref[rows(i, 1 - core)]


def pair_kernel(keep_ref, got_ref, out_ref):
    out_ref[...] = (keep_ref[...].astype(F32) + got_ref[...].astype(F32)).astype(BF16)


def sum_kernel(pieces_ref, out_ref):
    n, depth, _ = pieces_ref.shape
    total = pieces_ref[0].astype(F32)
    for i in range(1, n):
        total += pieces_ref[i].astype(F32)
    out_ref[...] = dot(total.astype(BF16), eye(depth), ((0,), (0,))).astype(BF16)


def mix_kernel(mix_ref, returned_ref, out_ref):
    rest = mix_ref[...]
    values = returned_ref[...]
    total = jnp.zeros(out_ref.shape, F32)
    for _ in range(3):
        piece = rest.astype(BF16)
        rest = rest - piece.astype(F32)
        total += dot(piece, values, ((1,), (0,)))
    out_ref[...] = total.astype(BF16)


def local(tokens, routes, route_weight, w_gate, w_up, w_down):
    experts, chips = lax.axis_size("expert"), lax.axis_size(GRID)
    rows, depth = tokens.shape
    capacity = min(rows, 2 * rows * routes.shape[1] // experts)
    slots = experts * capacity
    shape = jax.ShapeDtypeStruct
    swap = functools.partial(lax.ppermute, axis_name="core", perm=((0, 1), (1, 0)))

    placed, mix = call(
        functools.partial(place_kernel, capacity),
        (shape((slots, depth), BF16), shape((rows, slots), F32)),
        (tokens, routes, route_weight),
    )
    arrived = lax.all_to_all(placed.reshape(experts, capacity, depth), "expert", 0, 0, tiled=True)
    copies = call(turn_kernel, shape((chips, depth, slots), BF16), (arrived.reshape(slots, depth),))
    own = lax.all_to_all(copies, GRID, 0, 0, tiled=True)
    other = swap(own)
    core = lax.axis_index("core").astype(jnp.int32).reshape(1)
    operands = (own, other, core, w_gate[0], w_up[0], w_down[0])
    whole = 2 * chips * depth
    half = shape((chips, depth, slots), BF16)
    keep, send = pl.pallas_call(
        expert_kernel,
        out_shape=(half, half),
        in_specs=[VMEM, VMEM, pl.BlockSpec(memory_space=pltpu.SMEM), VMEM, VMEM, VMEM],
        out_specs=(VMEM, VMEM),
        scratch_shapes=[pltpu.VMEM((whole, slots), BF16), pltpu.VMEM((whole, slots), BF16)],
        compiler_params=pltpu.CompilerParams(vmem_limit_bytes=40 * 2**20),
    )(*operands)
    got = swap(send)
    paired = call(pair_kernel, half, (keep, got))
    pieces = lax.all_to_all(paired, GRID, 0, 0, tiled=True)
    summed = call(sum_kernel, shape((slots, depth), BF16), (pieces,))
    returned = lax.all_to_all(summed.reshape(experts, capacity, depth), "expert", 0, 0, tiled=True)
    return call(mix_kernel, shape((rows, depth), BF16), (mix, returned.reshape(slots, depth)))


def solution(mesh):
    chips_y = chips_x = 4
    devices = mesh.devices
    fine = Mesh(devices.reshape(devices.shape[0], chips_y, chips_x, 2), ("expert", "y", "x", "core"))
    tensor = ("y", "x", "core")
    placed = (
        P("expert", tensor),
        P("expert", None),
        P("expert", None),
        P("expert", tensor, None),
        P("expert", tensor, None),
        P("expert", tensor, None),
    )
    return jax.shard_map(local, mesh=fine, in_specs=placed, out_specs=P("expert", tensor), check_vma=False)
```

```python
import functools
import math

import jax
import jax.numpy as jnp
from jax import lax
from jax.experimental import pallas as pl
from jax.experimental.pallas import tpu as pltpu
from jax.sharding import Mesh, PartitionSpec as P

GRID = ("y", "x")
VMEM = pl.BlockSpec(memory_space=pltpu.VMEM)
BF16 = jnp.bfloat16
F32 = jnp.float32


def dot(left, right, dims, precision=None):
    return lax.dot_general(left, right, (dims, ((), ())), precision=precision, preferred_element_type=F32)


def eye(n):
    same = lax.broadcasted_iota(jnp.int32, (n, n), 0) == lax.broadcasted_iota(jnp.int32, (n, n), 1)
    return same.astype(F32).astype(BF16)


def call(body, out, operands, flops=0, core=None):
    scalar = () if core is None else (core,)
    specs = [pl.BlockSpec(memory_space=pltpu.SMEM)] * len(scalar) + [VMEM] * len(operands)
    moved = sum(math.prod(o.shape) * o.dtype.itemsize for o in (*operands, *jax.tree.leaves(out)))
    return pl.pallas_call(
        body,
        out_shape=out,
        in_specs=specs,
        out_specs=jax.tree.map(lambda _: VMEM, out),
        compiler_params=pltpu.CompilerParams(vmem_limit_bytes=40 * 2**20),
        cost_estimate=pl.CostEstimate(flops=flops, bytes_accessed=moved, transcendentals=0),
    )(*scalar, *operands)


def place_kernel(capacity, tokens_ref, routes_ref, weight_ref, placed_ref, mix_ref):
    top, rows = routes_ref.shape
    slots = placed_ref.shape[0]
    slot = lax.broadcasted_iota(jnp.int32, (slots, rows), 0)
    expert = slot // capacity
    spot = slot % capacity
    weight = weight_ref[...].astype(F32)
    share = weight / jnp.sum(weight, axis=0, keepdims=True)
    named = jnp.zeros((slots, rows), F32)
    mix = jnp.zeros((slots, rows), F32)
    for k in range(top):
        hit = routes_ref[k : k + 1, :] == expert
        named += jnp.where(hit, 1.0, 0.0)
        mix += jnp.where(hit, share[k : k + 1, :], 0.0)
    earlier = lax.broadcasted_iota(jnp.int32, (rows, rows), 0) < lax.broadcasted_iota(jnp.int32, (rows, rows), 1)
    before = dot(named.astype(BF16), earlier.astype(F32).astype(BF16), ((1,), (0,)))
    here = (named > 0.5) & (before.astype(jnp.int32) == spot)
    mix_ref[...] = jnp.where(here, mix, 0.0)
    dispatch = jnp.where(here, 1.0, 0.0).astype(BF16)
    placed_ref[...] = dot(dispatch, tokens_ref[...], ((1,), (0,))).astype(BF16)


def turn_kernel(arrived_ref, copies_ref):
    n, depth, _ = copies_ref.shape
    turned = dot(eye(depth), arrived_ref[...], ((1,), (1,))).astype(BF16)
    for i in range(n):
        copies_ref[i] = turned


def split_kernel(depth, core_ref, gate_ref, up_ref, down_ref, own_ref, send_ref):
    group = 4
    wide = 2 * group * depth
    thin = group * depth
    source = lax.broadcasted_iota(jnp.int32, (wide, thin), 0)
    target = lax.broadcasted_iota(jnp.int32, (wide, thin), 1)
    first = target + (target // depth) * depth
    own_pick = (source == first + core_ref[0] * depth).astype(F32).astype(BF16)
    send_pick = (source == first + (1 - core_ref[0]) * depth).astype(F32).astype(BF16)
    for k, ref in enumerate((gate_ref, up_ref, down_ref)):
        for g in range(ref.shape[1] // wide):
            block = ref[:, g * wide : (g + 1) * wide]
            own_ref[k, :, g * thin : (g + 1) * thin] = dot(block, own_pick, ((1,), (0,))).astype(BF16)
            send_ref[k, :, g * thin : (g + 1) * thin] = dot(block, send_pick, ((1,), (0,))).astype(BF16)


def stack_kernel(core_ref, own_ref, got_ref, rise_ref, fall_ref):
    units = own_ref.shape[1]
    pad = rise_ref.shape[1] - units
    for ref, which in ((own_ref, core_ref[0]), (got_ref, 1 - core_ref[0])):
        for k in range(2):
            rise_ref[2 * which + k, :units] = ref[k]
            rise_ref[2 * which + k, units:] = jnp.zeros((pad, rise_ref.shape[2]), BF16)
        fall_ref[which] = ref[2].T


def rise_kernel(x_ref, rise_ref, out_ref):
    n, units, slots = out_ref.shape
    padded = rise_ref.shape[0] // n
    product = dot(rise_ref[...], x_ref[...], ((1,), (0,)))
    for k in range(n):
        out_ref[k] = product[k * padded : k * padded + units].astype(BF16)


def fall_kernel(halves_ref, fall_ref, out_ref):
    hidden = []
    for u in range(2):
        gate = halves_ref[2 * u].astype(F32) + halves_ref[4 + 2 * u].astype(F32)
        up = halves_ref[2 * u + 1].astype(F32) + halves_ref[5 + 2 * u].astype(F32)
        hidden.append((gate / (1.0 + jnp.exp(-gate)) * up).astype(BF16))
    chunk = 384
    for i in range(out_ref.shape[0] // chunk):
        at = slice(i * chunk, (i + 1) * chunk)
        part = dot(fall_ref[0, at], hidden[0], ((1,), (0,))) + dot(fall_ref[1, at], hidden[1], ((1,), (0,)))
        out_ref[at] = part.astype(BF16)


def sum_kernel(pieces_ref, out_ref):
    n, depth, _ = pieces_ref.shape
    total = pieces_ref[0].astype(F32)
    for i in range(1, n):
        total += pieces_ref[i].astype(F32)
    out_ref[...] = dot(total.astype(BF16), eye(depth), ((0,), (0,))).astype(BF16)


def mix_kernel(mix_ref, returned_ref, out_ref):
    rest = mix_ref[...]
    values = returned_ref[...]
    total = jnp.zeros(out_ref.shape, F32)
    for _ in range(3):
        piece = rest.astype(BF16)
        rest = rest - piece.astype(F32)
        total += dot(piece, values, ((0,), (0,)))
    out_ref[...] = total.astype(BF16)


def local(tokens, routes, route_weight, w_gate, w_up, w_down):
    experts, chips = lax.axis_size("expert"), lax.axis_size(GRID)
    rows, depth = tokens.shape
    units, width = w_gate.shape[1:]
    half = width // 2
    padded = -(-units // 16) * 16
    capacity = min(rows, 2 * rows * routes.shape[1] // experts)
    slots = experts * capacity
    core = lax.axis_index("core").astype(jnp.int32).reshape(1)

    def shape(*dims, dtype=BF16):
        return jax.ShapeDtypeStruct(dims, dtype)

    placed, mix = call(
        functools.partial(place_kernel, capacity),
        (shape(slots, depth), shape(slots, rows, dtype=F32)),
        (tokens, routes.T, route_weight.T),
    )
    arrived = lax.all_to_all(placed.reshape(experts, capacity, depth), "expert", 0, 0, tiled=True)

    thirds = shape(3, units, half)
    own, send = call(
        functools.partial(split_kernel, depth),
        (thirds, thirds),
        (w_gate[0], w_up[0], w_down[0]),
        flops=3 * 2 * 2 * units * half * 8 * depth,
        core=core,
    )
    got = lax.ppermute(send, "core", ((0, 1), (1, 0)))
    rise, fall = call(stack_kernel, (shape(4, padded, half), shape(2, half, units)), (own, got), core=core)

    copies = call(turn_kernel, shape(chips, depth, slots), (arrived.reshape(slots, depth),))
    x = lax.all_to_all(copies, GRID, 0, 0, tiled=True).reshape(half, slots)
    partial = call(
        rise_kernel,
        shape(4, units, slots),
        (x, rise.reshape(4 * padded, half)),
        flops=2 * 4 * padded * half * slots,
    )
    halves = lax.all_gather(partial, "core", axis=0, tiled=True)
    part = call(fall_kernel, shape(half, slots), (halves, fall), flops=2 * 2 * units * half * slots)
    pieces = lax.all_to_all(part.reshape(chips, depth, slots), GRID, 0, 0, tiled=True)
    summed = call(sum_kernel, shape(slots, depth), (pieces,))
    returned = lax.all_to_all(summed.reshape(experts, capacity, depth), "expert", 0, 0, tiled=True)
    return call(mix_kernel, shape(rows, depth), (mix, returned.reshape(slots, depth)))


def solution(mesh):
    chips_y = chips_x = 4
    devices = mesh.devices
    fine = Mesh(devices.reshape(devices.shape[0], chips_y, chips_x, 2), ("expert", "y", "x", "core"))
    tensor = ("y", "x", "core")
    placed = (
        P("expert", tensor),
        P("expert", None),
        P("expert", None),
        P("expert", tensor, None),
        P("expert", tensor, None),
        P("expert", tensor, None),
    )
    return jax.shard_map(local, mesh=fine, in_specs=placed, out_specs=P("expert", tensor), check_vma=False)
```

```python
import functools
import math

import jax
import jax.numpy as jnp
from jax import lax
from jax.experimental import pallas as pl
from jax.experimental.pallas import tpu as pltpu
from jax.sharding import Mesh, PartitionSpec as P

GRID = ("y", "x")
VMEM = pl.BlockSpec(memory_space=pltpu.VMEM)
ANY = pl.BlockSpec(memory_space=pltpu.HBM)
BF16 = jnp.bfloat16
F32 = jnp.float32


def dot(left, right, dims, precision=None):
    return lax.dot_general(left, right, (dims, ((), ())), precision=precision, preferred_element_type=F32)


def eye(n):
    same = lax.broadcasted_iota(jnp.int32, (n, n), 0) == lax.broadcasted_iota(jnp.int32, (n, n), 1)
    return same.astype(F32).astype(BF16)


def call(body, out, operands, flops=0, core=None, far=(), aliases={}, far_out=0, scratch=(), cost=True, grant=20480):
    scalar = () if core is None else (core,)
    specs = [pl.BlockSpec(memory_space=pltpu.SMEM)] * len(scalar) + [VMEM] * len(operands) + [ANY] * len(far)
    outs = jax.tree.leaves(out)
    moved = sum(math.prod(o.shape) * o.dtype.itemsize for o in (*operands, *outs))
    out_specs = [VMEM] * (len(outs) - far_out) + [ANY] * far_out
    return pl.pallas_call(
        body,
        out_shape=out,
        in_specs=specs,
        out_specs=tuple(out_specs) if isinstance(out, tuple) else out_specs[0],
        input_output_aliases=aliases,
        scratch_shapes=list(scratch),
        compiler_params=pltpu.CompilerParams(vmem_limit_bytes=grant * 2**10),
        cost_estimate=pl.CostEstimate(flops=flops * cost, bytes_accessed=moved * cost, transcendentals=0),
    )(*scalar, *operands, *far)


def fetch(pairs, sems):
    copies = [pltpu.make_async_copy(source, target, sems.at[i]) for i, (source, target) in enumerate(pairs)]
    for copy in copies:
        copy.start()
    return copies


def place_kernel(capacity, tokens_far, routes_far, weight_far, placed_ref, mix_ref, tokens_ref, routes_ref, weight_ref, sems):
    pairs = ((tokens_far, tokens_ref), (routes_far, routes_ref), (weight_far, weight_ref))
    for copy in fetch(pairs, sems):
        copy.wait()
    top, rows = routes_ref.shape
    slots = placed_ref.shape[0]
    slot = lax.broadcasted_iota(jnp.int32, (slots, rows), 0)
    expert = slot // capacity
    spot = slot % capacity
    weight = weight_ref[...].astype(F32)
    share = weight / jnp.sum(weight, axis=0, keepdims=True)
    named = jnp.zeros((slots, rows), F32)
    mix = jnp.zeros((slots, rows), F32)
    for k in range(top):
        hit = routes_ref[k : k + 1, :] == expert
        named += jnp.where(hit, 1.0, 0.0)
        mix += jnp.where(hit, share[k : k + 1, :], 0.0)
    earlier = lax.broadcasted_iota(jnp.int32, (rows, rows), 0) < lax.broadcasted_iota(jnp.int32, (rows, rows), 1)
    before = dot(named.astype(BF16), earlier.astype(F32).astype(BF16), ((1,), (0,)))
    here = (named > 0.5) & (before.astype(jnp.int32) == spot)
    mix_ref[...] = jnp.where(here, mix, 0.0)
    dispatch = jnp.where(here, 1.0, 0.0).astype(BF16)
    placed_ref[...] = dot(dispatch, tokens_ref[...], ((1,), (0,))).astype(BF16)


def turn_kernel(arrived_ref, _, copies_ref, __):
    n, depth, _ = copies_ref.shape
    turned = dot(eye(depth), arrived_ref[...], ((1,), (1,))).astype(BF16)
    for i in range(n):
        copies_ref[i] = turned


def picker(depth, group, which):
    wide, thin = 2 * group * depth, group * depth
    source = lax.broadcasted_iota(jnp.int32, (wide, thin), 0)
    target = lax.broadcasted_iota(jnp.int32, (wide, thin), 1)
    return (source == target + (target // depth + which) * depth).astype(F32).astype(BF16)


def pick_kernel(depth, core_ref, gate_far, up_far, down_far, _, send_far, weights_ref, send_ref, sems, out_sems):
    loads = fetch([(far, weights_ref.at[k]) for k, far in enumerate((gate_far, up_far, down_far))], sems)
    wide, thin = 8 * depth, 4 * depth
    pick = picker(depth, 4, 1 - core_ref[0])
    stores = []
    for k, load in enumerate(loads):
        load.wait()
        for g in range(weights_ref.shape[2] // wide):
            block = weights_ref[k, :, g * wide : (g + 1) * wide]
            send_ref[k, :, g * thin : (g + 1) * thin] = dot(block, pick, ((1,), (0,))).astype(BF16)
        store = pltpu.make_async_copy(send_ref.at[k], send_far.at[k], out_sems.at[k])
        store.start()
        stores.append(store)
    for store in stores:
        store.wait()


def stack_kernel(
    depth, core_ref, gate_far, up_far, down_far, got_far, rise_ref, fall_far, weights_ref, got_ref, fall_ref, sems
):
    pairs = [(far, weights_ref.at[k]) for k, far in enumerate((gate_far, up_far, down_far))]
    loads = fetch(pairs + [(got_far.at[k], got_ref.at[k]) for k in range(3)], sems)
    units = got_ref.shape[1]
    pad = rise_ref.shape[1] - units
    wide, thin = 8 * depth, 4 * depth
    own, other = core_ref[0], 1 - core_ref[0]
    pick = picker(depth, 4, own)
    for k in range(4):
        rise_ref[k, units:] = jnp.zeros((pad, rise_ref.shape[2]), BF16)
    stores = [pltpu.make_async_copy(fall_ref.at[u], fall_far.at[u], sems.at[6 + i]) for i, u in enumerate((own, other))]
    for k in reversed(range(3)):
        loads[k].wait()
        for g in range(weights_ref.shape[2] // wide):
            block = weights_ref[k, :, g * wide : (g + 1) * wide]
            chosen = dot(block, pick, ((1,), (0,))).astype(BF16)
            if k < 2:
                rise_ref[2 * own + k, :units, g * thin : (g + 1) * thin] = chosen
            else:
                fall_ref[own, g * thin : (g + 1) * thin] = chosen.T
        if k == 2:
            stores[0].start()
    for k in reversed(range(3)):
        loads[3 + k].wait()
        if k < 2:
            rise_ref[2 * other + k, :units] = got_ref[k]
        else:
            fall_ref[other] = got_ref[k].T
            stores[1].start()
    for store in stores:
        store.wait()


def rise_kernel(x_ref, rise_ref, out_ref):
    n, units, slots = out_ref.shape
    padded = rise_ref.shape[0] // n
    product = dot(rise_ref[...], x_ref[...], ((1,), (0,)))
    for k in range(n):
        out_ref[k] = product[k * padded : k * padded + units].astype(BF16)


def fall_kernel(halves_ref, fall_ref, out_ref):
    hidden = []
    for u in range(2):
        gate = halves_ref[2 * u].astype(F32) + halves_ref[4 + 2 * u].astype(F32)
        up = halves_ref[2 * u + 1].astype(F32) + halves_ref[5 + 2 * u].astype(F32)
        hidden.append((gate / (1.0 + jnp.exp(-gate)) * up).astype(BF16))
    chunk = 384
    for i in range(out_ref.shape[0] // chunk):
        at = slice(i * chunk, (i + 1) * chunk)
        part = dot(fall_ref[0, at], hidden[0], ((1,), (0,))) + dot(fall_ref[1, at], hidden[1], ((1,), (0,)))
        out_ref[at] = part.astype(BF16)


def sum_kernel(pieces_ref, out_ref):
    n, depth, _ = pieces_ref.shape
    total = pieces_ref[0].astype(F32)
    for i in range(1, n):
        total += pieces_ref[i].astype(F32)
    out_ref[...] = dot(total.astype(BF16), eye(depth), ((0,), (0,))).astype(BF16)


def mix_kernel(mix_ref, returned_ref, out_ref):
    rest = mix_ref[...]
    values = returned_ref[...]
    total = jnp.zeros(out_ref.shape, F32)
    for _ in range(3):
        piece = rest.astype(BF16)
        rest = rest - piece.astype(F32)
        total += dot(piece, values, ((0,), (0,)))
    out_ref[...] = total.astype(BF16)


def local(tokens, routes, route_weight, w_gate, w_up, w_down):
    experts, chips = lax.axis_size("expert"), lax.axis_size(GRID)
    rows, depth = tokens.shape
    units, width = w_gate.shape[1:]
    half = width // 2
    padded = -(-units // 16) * 16
    capacity = min(rows, 2 * rows * routes.shape[1] // experts)
    slots = experts * capacity
    core = lax.axis_index("core").astype(jnp.int32).reshape(1)

    def shape(*dims, dtype=BF16):
        return jax.ShapeDtypeStruct(dims, dtype)

    placed, mix = call(
        functools.partial(place_kernel, capacity),
        (shape(slots, depth), shape(slots, rows, dtype=F32)),
        (),
        far=(tokens, routes.T, route_weight.T),
        scratch=(
            pltpu.VMEM(tokens.shape, tokens.dtype),
            pltpu.VMEM(routes.shape[::-1], routes.dtype),
            pltpu.VMEM(routes.shape[::-1], route_weight.dtype),
            pltpu.SemaphoreType.DMA((3,)),
        ),
        grant=65536,
    )
    arrived = lax.all_to_all(placed.reshape(experts, capacity, depth), "expert", 0, 0, tiled=True)

    weights = (w_gate[0], w_up[0], w_down[0])
    thirds = shape(3, units, half)
    whole_ref, third_ref = pltpu.VMEM((3, units, width), BF16), pltpu.VMEM(thirds.shape, BF16)
    picking = 3 * 2 * units * half * 8 * depth
    send = call(
        functools.partial(pick_kernel, depth),
        thirds,
        (),
        flops=picking,
        core=core,
        far=(*weights, placed),
        far_out=1,
        scratch=(whole_ref, third_ref, pltpu.SemaphoreType.DMA((3,)), pltpu.SemaphoreType.DMA((3,))),
        grant=65024,
    )
    copies, send = call(
        turn_kernel,
        (shape(chips, depth, slots), thirds),
        (arrived.reshape(slots, depth),),
        far=(send,),
        aliases={1: 1},
        far_out=1,
    )
    got = lax.ppermute(send, "core", ((0, 1), (1, 0)))
    rise, fall = call(
        functools.partial(stack_kernel, depth),
        (shape(4, padded, half), shape(2, half, units)),
        (),
        core=core,
        far=(*weights, got),
        far_out=1,
        scratch=(whole_ref, third_ref, pltpu.VMEM((2, half, units), BF16), pltpu.SemaphoreType.DMA((8,))),
        cost=False,
        grant=61440,
    )

    x = lax.all_to_all(copies, GRID, 0, 0, tiled=True).reshape(half, slots)
    partial = call(
        rise_kernel,
        shape(4, units, slots),
        (x, rise.reshape(4 * padded, half)),
        flops=2 * 4 * padded * half * slots,
    )
    halves = lax.all_gather(partial, "core", axis=0, tiled=True)
    part = call(fall_kernel, shape(half, slots), (halves, fall), flops=2 * 2 * units * half * slots)
    pieces = lax.all_to_all(part.reshape(chips, depth, slots), GRID, 0, 0, tiled=True)
    summed = call(sum_kernel, shape(slots, depth), (pieces,))
    returned = lax.all_to_all(summed.reshape(experts, capacity, depth), "expert", 0, 0, tiled=True)
    return call(mix_kernel, shape(rows, depth), (mix, returned.reshape(slots, depth)))


def solution(mesh):
    chips_y = chips_x = 4
    devices = mesh.devices
    fine = Mesh(devices.reshape(devices.shape[0], chips_y, chips_x, 2), ("expert", "y", "x", "core"))
    tensor = ("y", "x", "core")
    placed = (
        P("expert", tensor),
        P("expert", None),
        P("expert", None),
        P("expert", tensor, None),
        P("expert", tensor, None),
        P("expert", tensor, None),
    )
    return jax.shard_map(local, mesh=fine, in_specs=placed, out_specs=P("expert", tensor), check_vma=False)
```

```python
import functools
import math

import jax
import jax.numpy as jnp
from jax import lax
from jax.experimental import pallas as pl
from jax.experimental.pallas import tpu as pltpu
from jax.sharding import Mesh, PartitionSpec as P

GRID = ("y", "x")
VMEM = pl.BlockSpec(memory_space=pltpu.VMEM)
ANY = pl.BlockSpec(memory_space=pltpu.HBM)
BF16 = jnp.bfloat16
F32 = jnp.float32


def dot(left, right, dims, precision=None):
    return lax.dot_general(left, right, (dims, ((), ())), precision=precision, preferred_element_type=F32)


def eye(n):
    same = lax.broadcasted_iota(jnp.int32, (n, n), 0) == lax.broadcasted_iota(jnp.int32, (n, n), 1)
    return same.astype(F32).astype(BF16)


def call(body, out, operands, flops=0, core=None, far=(), far_out=0, scratch=(), grant=20480):
    scalar = () if core is None else (core,)
    specs = [pl.BlockSpec(memory_space=pltpu.SMEM)] * len(scalar) + [VMEM] * len(operands) + [ANY] * len(far)
    outs = jax.tree.leaves(out)
    moved = sum(math.prod(o.shape) * o.dtype.itemsize for o in (*operands, *outs))
    out_specs = [VMEM] * (len(outs) - far_out) + [ANY] * far_out
    return pl.pallas_call(
        body,
        out_shape=out,
        in_specs=specs,
        out_specs=tuple(out_specs) if isinstance(out, tuple) else out_specs[0],
        scratch_shapes=list(scratch),
        compiler_params=pltpu.CompilerParams(vmem_limit_bytes=grant * 2**10),
        cost_estimate=pl.CostEstimate(flops=flops, bytes_accessed=moved, transcendentals=0),
    )(*scalar, *operands, *far)


def fetch(pairs, sems):
    copies = [pltpu.make_async_copy(source, target, sems.at[i]) for i, (source, target) in enumerate(pairs)]
    for copy in copies:
        copy.start()
    return copies


def place_kernel(capacity, tokens_far, routes_far, weight_far, placed_ref, mix_ref, tokens_ref, routes_ref, weight_ref, sems):
    pairs = ((tokens_far, tokens_ref), (routes_far, routes_ref), (weight_far, weight_ref))
    for copy in fetch(pairs, sems):
        copy.wait()
    top, rows = routes_ref.shape
    slots = placed_ref.shape[0]
    slot = lax.broadcasted_iota(jnp.int32, (slots, rows), 0)
    expert = slot // capacity
    spot = slot % capacity
    weight = weight_ref[...].astype(F32)
    share = weight / jnp.sum(weight, axis=0, keepdims=True)
    named = jnp.zeros((slots, rows), F32)
    mix = jnp.zeros((slots, rows), F32)
    for k in range(top):
        hit = routes_ref[k : k + 1, :] == expert
        named += jnp.where(hit, 1.0, 0.0)
        mix += jnp.where(hit, share[k : k + 1, :], 0.0)
    earlier = lax.broadcasted_iota(jnp.int32, (rows, rows), 0) < lax.broadcasted_iota(jnp.int32, (rows, rows), 1)
    before = dot(named.astype(BF16), earlier.astype(F32).astype(BF16), ((1,), (0,)))
    here = (named > 0.5) & (before.astype(jnp.int32) == spot)
    mix_ref[...] = jnp.where(here, mix, 0.0)
    dispatch = jnp.where(here, 1.0, 0.0).astype(BF16)
    placed_ref[...] = dot(dispatch, tokens_ref[...], ((1,), (0,))).astype(BF16)


def turn_kernel(arrived_ref, copies_ref):
    n, depth, _ = copies_ref.shape
    turned = dot(eye(depth), arrived_ref[...], ((1,), (1,))).astype(BF16)
    for i in range(n):
        copies_ref[i] = turned


def pick_kernel(depth, core_ref, gate_far, up_far, down_far, _, send_far, weights_ref, send_ref, sems, out_sems):
    loads = fetch([(far, weights_ref.at[k]) for k, far in enumerate((gate_far, up_far, down_far))], sems)
    wide, thin = 8 * depth, 4 * depth
    stores = []
    for k, load in enumerate(loads):
        load.wait()
        for which in range(2):

            @pl.when(core_ref[0] != which)
            def _():
                for g in range(weights_ref.shape[2] // wide):
                    starts = [g * wide + (2 * i + which) * depth for i in range(4)]
                    pieces = [weights_ref[k, :, start : start + depth] for start in starts]
                    send_ref[k, :, g * thin : (g + 1) * thin] = jnp.concatenate(pieces, axis=1)

        store = pltpu.make_async_copy(send_ref.at[k], send_far.at[k], out_sems.at[k])
        store.start()
        stores.append(store)
    for store in stores:
        store.wait()


def rise_kernel(core_ref, x_ref, gate_ref, up_ref, got_ref, out_ref, spread_ref):
    own, other = core_ref[0], 1 - core_ref[0]
    n, depth, _ = x_ref.shape
    for i in range(n):
        spread_ref[pl.ds(pl.multiple_of((2 * i + own) * depth, depth), depth)] = x_ref[i]
        spread_ref[pl.ds(pl.multiple_of((2 * i + other) * depth, depth), depth)] = jnp.zeros_like(x_ref[i])
    x = x_ref[...].reshape(n * depth, x_ref.shape[2])
    for k, ref in enumerate((gate_ref, up_ref)):
        out_ref[2 * own + k] = dot(ref[...], spread_ref[...], ((1,), (0,))).astype(BF16)
        out_ref[2 * other + k] = dot(got_ref[k], x, ((1,), (0,))).astype(BF16)


def fall_kernel(core_ref, halves_ref, down_ref, got_ref, out_ref, part_ref):
    own, other = core_ref[0], 1 - core_ref[0]
    n, depth, _ = out_ref.shape
    hidden = []
    for u in (own, other):
        gate = halves_ref[2 * u].astype(F32) + halves_ref[4 + 2 * u].astype(F32)
        up = halves_ref[2 * u + 1].astype(F32) + halves_ref[5 + 2 * u].astype(F32)
        hidden.append((gate / (1.0 + jnp.exp(-gate)) * up).astype(BF16))
    part_ref[...] = dot(down_ref[...], hidden[0], ((0,), (0,)))
    group = 4
    for g in range(n // group):
        columns = slice(g * group * depth, (g + 1) * group * depth)
        rest = dot(got_ref[2, :, columns], hidden[1], ((0,), (0,)))
        for j in range(group):
            i = g * group + j
            first = part_ref[pl.ds(pl.multiple_of((2 * i + own) * depth, depth), depth)]
            out_ref[i] = (first + rest[j * depth : (j + 1) * depth]).astype(BF16)


def sum_kernel(pieces_ref, out_ref):
    n, depth, _ = pieces_ref.shape
    total = pieces_ref[0].astype(F32)
    for i in range(1, n):
        total += pieces_ref[i].astype(F32)
    out_ref[...] = dot(total.astype(BF16), eye(depth), ((0,), (0,))).astype(BF16)


def mix_kernel(mix_ref, returned_ref, out_ref):
    rest = mix_ref[...]
    values = returned_ref[...]
    total = jnp.zeros(out_ref.shape, F32)
    for _ in range(3):
        piece = rest.astype(BF16)
        rest = rest - piece.astype(F32)
        total += dot(piece, values, ((0,), (0,)))
    out_ref[...] = total.astype(BF16)


def local(tokens, routes, route_weight, w_gate, w_up, w_down):
    experts, chips = lax.axis_size("expert"), lax.axis_size(GRID)
    rows, depth = tokens.shape
    units, width = w_gate.shape[1:]
    half = width // 2
    padded = -(-units // 16) * 16
    capacity = min(rows, 2 * rows * routes.shape[1] // experts)
    slots = experts * capacity
    core = lax.axis_index("core").astype(jnp.int32).reshape(1)

    def shape(*dims, dtype=BF16):
        return jax.ShapeDtypeStruct(dims, dtype)

    placed, mix = call(
        functools.partial(place_kernel, capacity),
        (shape(slots, depth), shape(slots, rows, dtype=F32)),
        (),
        far=(tokens, routes.T, route_weight.T),
        scratch=(
            pltpu.VMEM(tokens.shape, tokens.dtype),
            pltpu.VMEM(routes.shape[::-1], routes.dtype),
            pltpu.VMEM(routes.shape[::-1], route_weight.dtype),
            pltpu.SemaphoreType.DMA((3,)),
        ),
        grant=65536,
    )
    arrived = lax.all_to_all(placed.reshape(experts, capacity, depth), "expert", 0, 0, tiled=True)

    weights = (w_gate[0], w_up[0], w_down[0])
    thirds = shape(3, units, half)
    whole_ref, third_ref = pltpu.VMEM((3, units, width), BF16), pltpu.VMEM(thirds.shape, BF16)
    send = call(
        functools.partial(pick_kernel, depth),
        thirds,
        (),
        flops=10**8,
        core=core,
        far=(*weights, placed),
        far_out=1,
        scratch=(whole_ref, third_ref, pltpu.SemaphoreType.DMA((3,)), pltpu.SemaphoreType.DMA((3,))),
        grant=65024,
    )
    got = lax.ppermute(send, "core", ((0, 1), (1, 0)))
    copies = call(turn_kernel, shape(chips, depth, slots), (arrived.reshape(slots, depth),), flops=10**11)
    x = lax.all_to_all(copies, GRID, 0, 0, tiled=True)
    partial = call(
        rise_kernel,
        shape(4, units, slots),
        (x, *weights[:2], got),
        flops=2 * 6 * units * half * slots,
        core=core,
        scratch=(pltpu.VMEM((width, slots), BF16),),
    )
    halves = lax.all_gather(partial, "core", axis=0, tiled=True)
    part = call(
        fall_kernel,
        shape(chips, depth, slots),
        (halves, weights[2], got),
        flops=2 * 3 * units * half * slots,
        core=core,
        scratch=(pltpu.VMEM((width, slots), F32),),
    )
    pieces = lax.all_to_all(part, GRID, 0, 0, tiled=True)
    summed = call(sum_kernel, shape(slots, depth), (pieces,))
    returned = lax.all_to_all(summed.reshape(experts, capacity, depth), "expert", 0, 0, tiled=True)
    return call(mix_kernel, shape(rows, depth), (mix, returned.reshape(slots, depth)))


def solution(mesh):
    chips_y = chips_x = 4
    devices = mesh.devices
    fine = Mesh(devices.reshape(devices.shape[0], chips_y, chips_x, 2), ("expert", "y", "x", "core"))
    tensor = ("y", "x", "core")
    placed = (
        P("expert", tensor),
        P("expert", None),
        P("expert", None),
        P("expert", tensor, None),
        P("expert", tensor, None),
        P("expert", tensor, None),
    )
    return jax.shard_map(local, mesh=fine, in_specs=placed, out_specs=P("expert", tensor), check_vma=False)
```

```python
import functools
import math

import jax
import jax.numpy as jnp
from jax import lax
from jax.experimental import pallas as pl
from jax.experimental.pallas import tpu as pltpu
from jax.sharding import PartitionSpec as P

VMEM = pl.BlockSpec(memory_space=pltpu.VMEM)
ANY = pl.BlockSpec(memory_space=pltpu.HBM)
BF16 = jnp.bfloat16
F32 = jnp.float32
FIRST, LAST = 11, 8


def dot(left, right, dims, precision=None):
    return lax.dot_general(left, right, (dims, ((), ())), precision=precision, preferred_element_type=F32)


def eye(n):
    same = lax.broadcasted_iota(jnp.int32, (n, n), 0) == lax.broadcasted_iota(jnp.int32, (n, n), 1)
    return same.astype(F32).astype(BF16)


def store_turned(ref, value, shift):
    cut = shift % value.shape[0]
    ref[: value.shape[0] - cut] = value[cut:]
    if cut:
        ref[value.shape[0] - cut :] = value[:cut]


def chip_at(i, n):
    return (i + n - 1) % n


def call(body, out, operands, flops=0, core=None, far=(), far_out=0, scratch=(), grant=20480):
    scalar = () if core is None else (core,)
    specs = [pl.BlockSpec(memory_space=pltpu.SMEM)] * len(scalar) + [VMEM] * len(operands) + [ANY] * len(far)
    outs = jax.tree.leaves(out)
    moved = sum(math.prod(o.shape) * o.dtype.itemsize for o in (*operands, *outs))
    out_specs = [VMEM] * (len(outs) - far_out) + [ANY] * far_out
    return pl.pallas_call(
        body,
        out_shape=out,
        in_specs=specs,
        out_specs=tuple(out_specs) if isinstance(out, tuple) else out_specs[0],
        scratch_shapes=list(scratch),
        compiler_params=pltpu.CompilerParams(vmem_limit_bytes=grant * 2**10),
        cost_estimate=pl.CostEstimate(flops=flops, bytes_accessed=moved, transcendentals=0),
    )(*scalar, *operands, *far)


def fetch(pairs, sems):
    copies = [pltpu.make_async_copy(source, target, sems.at[i]) for i, (source, target) in enumerate(pairs)]
    for copy in copies:
        copy.start()
    return copies


def place_kernel(capacity, first, shift, tokens_far, routes_far, weight_far, placed_ref, mix_ref, tokens_ref, routes_ref, weight_ref, sems):
    pairs = ((tokens_far, tokens_ref), (routes_far, routes_ref), (weight_far, weight_ref))
    for copy in fetch(pairs, sems):
        copy.wait()
    top, rows = routes_ref.shape
    slots = placed_ref.shape[0]
    slot = lax.broadcasted_iota(jnp.int32, (slots, rows), 0)
    experts = slots // capacity
    expert = (slot // capacity + first) % experts
    spot = slot % capacity
    weight = weight_ref[...].astype(F32)
    share = weight / jnp.sum(weight, axis=0, keepdims=True)
    named = jnp.zeros((slots, rows), F32)
    mix = jnp.zeros((slots, rows), F32)
    for k in range(top):
        hit = routes_ref[k : k + 1, :] == expert
        named += jnp.where(hit, 1.0, 0.0)
        mix += jnp.where(hit, share[k : k + 1, :], 0.0)
    earlier = lax.broadcasted_iota(jnp.int32, (rows, rows), 0) < lax.broadcasted_iota(jnp.int32, (rows, rows), 1)
    before = dot(named.astype(BF16), earlier.astype(F32).astype(BF16), ((1,), (0,)))
    here = (named > 0.5) & (before.astype(jnp.int32) == spot)
    store_turned(mix_ref, jnp.where(here, mix, 0.0), shift)
    dispatch = jnp.where(here, 1.0, 0.0).astype(BF16)
    placed_ref[...] = dot(dispatch, tokens_ref[...], ((1,), (0,))).astype(BF16)


def turn_kernel(arrived_ref, copies_ref):
    n, depth, _ = copies_ref.shape
    turned = dot(eye(depth), arrived_ref[...], ((1,), (1,))).astype(BF16)
    for i in range(n):
        copies_ref[i] = turned


def pick_kernel(depth, core_ref, gate_far, up_far, down_far, _, send_far, weights_ref, send_ref, sems, out_sems):
    loads = fetch([(far, weights_ref.at[k]) for k, far in enumerate((gate_far, up_far, down_far))], sems)
    n = weights_ref.shape[2] // (2 * depth)
    thin = 4 * depth
    stores = []
    for k, load in enumerate(loads):
        load.wait()
        for which in range(2):

            @pl.when(core_ref[0] != which)
            def _():
                for g in range(n // 4):
                    starts = [(2 * chip_at(4 * g + i, n) + which) * depth for i in range(4)]
                    pieces = [weights_ref[k, :, start : start + depth] for start in starts]
                    send_ref[k, :, g * thin : (g + 1) * thin] = jnp.concatenate(pieces, axis=1)

        store = pltpu.make_async_copy(send_ref.at[k], send_far.at[k], out_sems.at[k])
        store.start()
        stores.append(store)
    for store in stores:
        store.wait()


def rise_kernel(core_ref, x_ref, gate_ref, up_ref, got_ref, out_ref, spread_ref):
    own, other = core_ref[0], 1 - core_ref[0]
    n, depth, _ = x_ref.shape
    for i in range(n):
        chip = chip_at(i, n)
        spread_ref[pl.ds(pl.multiple_of((2 * chip + own) * depth, depth), depth)] = x_ref[i]
        spread_ref[pl.ds(pl.multiple_of((2 * chip + other) * depth, depth), depth)] = jnp.zeros_like(x_ref[i])
    x = x_ref[...].reshape(n * depth, x_ref.shape[2])
    for k, ref in enumerate((gate_ref, up_ref)):
        out_ref[2 * own + k] = dot(ref[...], spread_ref[...], ((1,), (0,))).astype(BF16)
        out_ref[2 * other + k] = dot(got_ref[k], x, ((1,), (0,))).astype(BF16)


def fall_kernel(core_ref, halves_ref, down_ref, got_ref, out_ref, part_ref):
    own, other = core_ref[0], 1 - core_ref[0]
    n, depth, _ = out_ref.shape
    hidden = []
    for u in (own, other):
        gate = halves_ref[2 * u].astype(F32) + halves_ref[4 + 2 * u].astype(F32)
        up = halves_ref[2 * u + 1].astype(F32) + halves_ref[5 + 2 * u].astype(F32)
        hidden.append((gate / (1.0 + jnp.exp(-gate)) * up).astype(BF16))
    part_ref[...] = dot(down_ref[...], hidden[0], ((0,), (0,)))
    group = 4
    for g in range(n // group):
        columns = slice(g * group * depth, (g + 1) * group * depth)
        rest = dot(got_ref[2, :, columns], hidden[1], ((0,), (0,)))
        for j in range(group):
            i = g * group + j
            first = part_ref[pl.ds(pl.multiple_of((2 * chip_at(i, n) + own) * depth, depth), depth)]
            out_ref[i] = (first + rest[j * depth : (j + 1) * depth]).astype(BF16)


def sum_kernel(shift, pieces_ref, out_ref):
    n, depth, _ = pieces_ref.shape
    total = pieces_ref[0].astype(F32)
    for i in range(1, n):
        total += pieces_ref[i].astype(F32)
    store_turned(out_ref, dot(total.astype(BF16), eye(depth), ((0,), (0,))).astype(BF16), shift)


def mix_kernel(mix_ref, returned_ref, out_ref):
    rest = mix_ref[...]
    values = returned_ref[...]
    total = jnp.zeros(out_ref.shape, F32)
    for _ in range(3):
        piece = rest.astype(BF16)
        rest = rest - piece.astype(F32)
        total += dot(piece, values, ((0,), (0,)))
    out_ref[...] = total.astype(BF16)


def local(tokens, routes, route_weight, w_gate, w_up, w_down):
    experts, chips = lax.axis_size("expert"), lax.axis_size("tensor") // 2
    rows, depth = tokens.shape
    units, width = w_gate.shape[1:]
    half = width // 2
    padded = -(-units // 16) * 16
    capacity = min(rows, 2 * rows * routes.shape[1] // experts)
    slots = experts * capacity
    first, last = FIRST * experts // 16, LAST * experts // 16
    order_out = [[(i + first) % experts for i in range(experts)]]
    order_back = [[(i + last) % experts for i in range(experts)]]
    shift = (last - first) * capacity
    same_core = [[2 * chip_at(i, chips) + c for i in range(chips)] for c in range(2)]
    same_chip = [[2 * i, 2 * i + 1] for i in range(chips)]
    core = (lax.axis_index("tensor") % 2).astype(jnp.int32).reshape(1)

    def shape(*dims, dtype=BF16):
        return jax.ShapeDtypeStruct(dims, dtype)

    placed, mix = call(
        functools.partial(place_kernel, capacity, first, shift),
        (shape(slots, depth), shape(slots, rows, dtype=F32)),
        (),
        far=(tokens, routes.T, route_weight.T),
        scratch=(
            pltpu.VMEM(tokens.shape, tokens.dtype),
            pltpu.VMEM(routes.shape[::-1], routes.dtype),
            pltpu.VMEM(routes.shape[::-1], route_weight.dtype),
            pltpu.SemaphoreType.DMA((3,)),
        ),
        grant=65536,
    )
    arrived = lax.all_to_all(placed.reshape(experts, capacity, depth), "expert", 0, 0, axis_index_groups=order_out, tiled=True)

    weights = (w_gate[0], w_up[0], w_down[0])
    thirds = shape(3, units, half)
    whole_ref, third_ref = pltpu.VMEM((3, units, width), BF16), pltpu.VMEM(thirds.shape, BF16)
    send = call(
        functools.partial(pick_kernel, depth),
        thirds,
        (),
        flops=10**8,
        core=core,
        far=(*weights, placed),
        far_out=1,
        scratch=(whole_ref, third_ref, pltpu.SemaphoreType.DMA((3,)), pltpu.SemaphoreType.DMA((3,))),
        grant=65024,
    )
    got = lax.ppermute(send, "tensor", [(i, i ^ 1) for i in range(2 * chips)])
    copies = call(turn_kernel, shape(chips, depth, slots), (arrived.reshape(slots, depth),), flops=10**11)
    x = lax.all_to_all(copies, "tensor", 0, 0, axis_index_groups=same_core, tiled=True)
    partial = call(
        rise_kernel,
        shape(4, units, slots),
        (x, *weights[:2], got),
        flops=2 * 6 * units * half * slots,
        core=core,
        scratch=(pltpu.VMEM((width, slots), BF16),),
    )
    halves = lax.all_gather(partial, "tensor", axis=0, axis_index_groups=same_chip, tiled=True)
    part = call(
        fall_kernel,
        shape(chips, depth, slots),
        (halves, weights[2], got),
        flops=2 * 3 * units * half * slots,
        core=core,
        scratch=(pltpu.VMEM((width, slots), F32),),
    )
    pieces = lax.all_to_all(part, "tensor", 0, 0, axis_index_groups=same_core, tiled=True)
    summed = call(functools.partial(sum_kernel, shift), shape(slots, depth), (pieces,))
    returned = lax.all_to_all(summed.reshape(experts, capacity, depth), "expert", 0, 0, axis_index_groups=order_back, tiled=True)
    return call(mix_kernel, shape(rows, depth), (mix, returned.reshape(slots, depth)))


def solution(mesh):
    placed = (
        P("expert", "tensor"),
        P("expert", None),
        P("expert", None),
        P("expert", "tensor", None),
        P("expert", "tensor", None),
        P("expert", "tensor", None),
    )
    return jax.shard_map(local, mesh=mesh, in_specs=placed, out_specs=P("expert", "tensor"), check_vma=False)
```

```python
import functools
import math

import jax
import jax.numpy as jnp
from jax import lax
from jax.experimental import pallas as pl
from jax.experimental.pallas import tpu as pltpu
from jax.sharding import PartitionSpec as P

VMEM = pl.BlockSpec(memory_space=pltpu.VMEM)
ANY = pl.BlockSpec(memory_space=pltpu.HBM)
BF16 = jnp.bfloat16
F32 = jnp.float32
FIRST, LAST, CHIP = 11, 8, 10


def dot(left, right, dims, precision=None):
    return lax.dot_general(left, right, (dims, ((), ())), precision=precision, preferred_element_type=F32)


def eye(n):
    same = lax.broadcasted_iota(jnp.int32, (n, n), 0) == lax.broadcasted_iota(jnp.int32, (n, n), 1)
    return same.astype(F32).astype(BF16)


def store_turned(ref, value, shift):
    cut = shift % value.shape[0]
    ref[: value.shape[0] - cut] = value[cut:]
    if cut:
        ref[value.shape[0] - cut :] = value[:cut]


def chip_at(i, n):
    return (i + CHIP * n // 16) % n


def call(body, out, operands, flops=0, core=None, far=(), far_out=0, scratch=(), grant=20480):
    scalar = () if core is None else (core,)
    specs = [pl.BlockSpec(memory_space=pltpu.SMEM)] * len(scalar) + [VMEM] * len(operands) + [ANY] * len(far)
    outs = jax.tree.leaves(out)
    moved = sum(math.prod(o.shape) * o.dtype.itemsize for o in (*operands, *outs))
    out_specs = [VMEM] * (len(outs) - far_out) + [ANY] * far_out
    return pl.pallas_call(
        body,
        out_shape=out,
        in_specs=specs,
        out_specs=tuple(out_specs) if isinstance(out, tuple) else out_specs[0],
        scratch_shapes=list(scratch),
        compiler_params=pltpu.CompilerParams(vmem_limit_bytes=grant * 2**10),
        cost_estimate=pl.CostEstimate(flops=flops, bytes_accessed=moved, transcendentals=0),
    )(*scalar, *operands, *far)


def fetch(pairs, sems):
    copies = [pltpu.make_async_copy(source, target, sems.at[i]) for i, (source, target) in enumerate(pairs)]
    for copy in copies:
        copy.start()
    return copies


def place_kernel(capacity, first, shift, tokens_far, routes_far, weight_far, placed_ref, mix_ref, tokens_ref, routes_ref, weight_ref, sems):
    pairs = ((tokens_far, tokens_ref), (routes_far, routes_ref), (weight_far, weight_ref))
    for copy in fetch(pairs, sems):
        copy.wait()
    top, rows = routes_ref.shape
    slots = placed_ref.shape[0]
    slot = lax.broadcasted_iota(jnp.int32, (slots, rows), 0)
    experts = slots // capacity
    expert = (slot // capacity + first) % experts
    spot = slot % capacity
    weight = weight_ref[...].astype(F32)
    share = weight / jnp.sum(weight, axis=0, keepdims=True)
    named = jnp.zeros((slots, rows), F32)
    mix = jnp.zeros((slots, rows), F32)
    for k in range(top):
        hit = routes_ref[k : k + 1, :] == expert
        named += jnp.where(hit, 1.0, 0.0)
        mix += jnp.where(hit, share[k : k + 1, :], 0.0)
    earlier = lax.broadcasted_iota(jnp.int32, (rows, rows), 0) < lax.broadcasted_iota(jnp.int32, (rows, rows), 1)
    before = dot(named.astype(BF16), earlier.astype(F32).astype(BF16), ((1,), (0,)))
    here = (named > 0.5) & (before.astype(jnp.int32) == spot)
    store_turned(mix_ref, jnp.where(here, mix, 0.0), shift)
    dispatch = jnp.where(here, 1.0, 0.0).astype(BF16)
    placed_ref[...] = dot(dispatch, tokens_ref[...], ((1,), (0,))).astype(BF16)


def turn_kernel(arrived_ref, copies_ref):
    n, depth, _ = copies_ref.shape
    turned = dot(eye(depth), arrived_ref[...], ((1,), (1,))).astype(BF16)
    for i in range(n):
        copies_ref[i] = turned


def pick_kernel(depth, core_ref, gate_far, up_far, down_far, _, send_far, weights_ref, send_ref, sems, out_sems):
    loads = fetch([(far, weights_ref.at[k]) for k, far in enumerate((gate_far, up_far, down_far))], sems)
    n = weights_ref.shape[2] // (2 * depth)
    thin = 4 * depth
    stores = []
    for k, load in enumerate(loads):
        load.wait()
        for which in range(2):

            @pl.when(core_ref[0] != which)
            def _():
                for g in range(n // 4):
                    starts = [(2 * chip_at(4 * g + i, n) + which) * depth for i in range(4)]
                    pieces = [weights_ref[k, :, start : start + depth] for start in starts]
                    send_ref[k, :, g * thin : (g + 1) * thin] = jnp.concatenate(pieces, axis=1)

        store = pltpu.make_async_copy(send_ref.at[k], send_far.at[k], out_sems.at[k])
        store.start()
        stores.append(store)
    for store in stores:
        store.wait()


def rise_kernel(core_ref, x_ref, gate_ref, up_ref, got_ref, out_ref, spread_ref):
    own, other = core_ref[0], 1 - core_ref[0]
    n, depth, _ = x_ref.shape
    for i in range(n):
        chip = chip_at(i, n)
        spread_ref[pl.ds(pl.multiple_of((2 * chip + own) * depth, depth), depth)] = x_ref[i]
        spread_ref[pl.ds(pl.multiple_of((2 * chip + other) * depth, depth), depth)] = jnp.zeros_like(x_ref[i])
    x = x_ref[...].reshape(n * depth, x_ref.shape[2])
    for k, ref in enumerate((gate_ref, up_ref)):
        out_ref[2 * own + k] = dot(ref[...], spread_ref[...], ((1,), (0,))).astype(BF16)
        out_ref[2 * other + k] = dot(got_ref[k], x, ((1,), (0,))).astype(BF16)


def fall_kernel(core_ref, halves_ref, down_ref, got_ref, out_ref, part_ref):
    own, other = core_ref[0], 1 - core_ref[0]
    n, depth, _ = out_ref.shape
    hidden = []
    for u in (own, other):
        gate = halves_ref[2 * u].astype(F32) + halves_ref[4 + 2 * u].astype(F32)
        up = halves_ref[2 * u + 1].astype(F32) + halves_ref[5 + 2 * u].astype(F32)
        hidden.append((gate / (1.0 + jnp.exp(-gate)) * up).astype(BF16))
    part_ref[...] = dot(down_ref[...], hidden[0], ((0,), (0,)))
    group = 4
    for g in range(n // group):
        columns = slice(g * group * depth, (g + 1) * group * depth)
        rest = dot(got_ref[2, :, columns], hidden[1], ((0,), (0,)))
        for j in range(group):
            i = g * group + j
            first = part_ref[pl.ds(pl.multiple_of((2 * chip_at(i, n) + own) * depth, depth), depth)]
            out_ref[i] = (first + rest[j * depth : (j + 1) * depth]).astype(BF16)


def sum_kernel(shift, pieces_ref, out_ref):
    n, depth, _ = pieces_ref.shape
    total = pieces_ref[0].astype(F32)
    for i in range(1, n):
        total += pieces_ref[i].astype(F32)
    store_turned(out_ref, dot(total.astype(BF16), eye(depth), ((0,), (0,))).astype(BF16), shift)


def mix_kernel(mix_ref, returned_ref, out_ref):
    rest = mix_ref[...]
    values = returned_ref[...]
    total = jnp.zeros(out_ref.shape, F32)
    for _ in range(3):
        piece = rest.astype(BF16)
        rest = rest - piece.astype(F32)
        total += dot(piece, values, ((0,), (0,)))
    out_ref[...] = total.astype(BF16)


def local(tokens, routes, route_weight, w_gate, w_up, w_down):
    experts, chips = lax.axis_size("expert"), lax.axis_size("tensor") // 2
    rows, depth = tokens.shape
    units, width = w_gate.shape[1:]
    half = width // 2
    padded = -(-units // 16) * 16
    capacity = min(rows, 2 * rows * routes.shape[1] // experts)
    slots = experts * capacity
    first, last = FIRST * experts // 16, LAST * experts // 16
    order_out = [[(i + first) % experts for i in range(experts)]]
    order_back = [[(i + last) % experts for i in range(experts)]]
    shift = (last - first) * capacity
    same_core = [[2 * chip_at(i, chips) + c for i in range(chips)] for c in range(2)]
    same_chip = [[2 * i, 2 * i + 1] for i in range(chips)]
    core = (lax.axis_index("tensor") % 2).astype(jnp.int32).reshape(1)

    def shape(*dims, dtype=BF16):
        return jax.ShapeDtypeStruct(dims, dtype)

    placed, mix = call(
        functools.partial(place_kernel, capacity, first, shift),
        (shape(slots, depth), shape(slots, rows, dtype=F32)),
        (),
        far=(tokens, routes.T, route_weight.T),
        scratch=(
            pltpu.VMEM(tokens.shape, tokens.dtype),
            pltpu.VMEM(routes.shape[::-1], routes.dtype),
            pltpu.VMEM(routes.shape[::-1], route_weight.dtype),
            pltpu.SemaphoreType.DMA((3,)),
        ),
        grant=65536,
    )
    arrived = lax.all_to_all(placed.reshape(experts, capacity, depth), "expert", 0, 0, axis_index_groups=order_out, tiled=True)

    weights = (w_gate[0], w_up[0], w_down[0])
    thirds = shape(3, units, half)
    whole_ref, third_ref = pltpu.VMEM((3, units, width), BF16), pltpu.VMEM(thirds.shape, BF16)
    send = call(
        functools.partial(pick_kernel, depth),
        thirds,
        (),
        flops=10**8,
        core=core,
        far=(*weights, placed),
        far_out=1,
        scratch=(whole_ref, third_ref, pltpu.SemaphoreType.DMA((3,)), pltpu.SemaphoreType.DMA((3,))),
        grant=65024,
    )
    got = lax.ppermute(send, "tensor", [(i, i ^ 1) for i in range(2 * chips)])
    copies = call(turn_kernel, shape(chips, depth, slots), (arrived.reshape(slots, depth),), flops=10**11)
    x = lax.all_to_all(copies, "tensor", 0, 0, axis_index_groups=same_core, tiled=True)
    partial = call(
        rise_kernel,
        shape(4, units, slots),
        (x, *weights[:2], got),
        flops=2 * 6 * units * half * slots,
        core=core,
        scratch=(pltpu.VMEM((width, slots), BF16),),
    )
    halves = lax.all_gather(partial, "tensor", axis=0, axis_index_groups=same_chip, tiled=True)
    part = call(
        fall_kernel,
        shape(chips, depth, slots),
        (halves, weights[2], got),
        flops=2 * 3 * units * half * slots,
        core=core,
        scratch=(pltpu.VMEM((width, slots), F32),),
    )
    pieces = lax.all_to_all(part, "tensor", 0, 0, axis_index_groups=same_core, tiled=True)
    summed = call(functools.partial(sum_kernel, shift), shape(slots, depth), (pieces,))
    returned = lax.all_to_all(summed.reshape(experts, capacity, depth), "expert", 0, 0, axis_index_groups=order_back, tiled=True)
    return call(mix_kernel, shape(rows, depth), (mix, returned.reshape(slots, depth)))


def solution(mesh):
    placed = (
        P("expert", "tensor"),
        P("expert", None),
        P("expert", None),
        P("expert", "tensor", None),
        P("expert", "tensor", None),
        P("expert", "tensor", None),
    )
    return jax.shard_map(local, mesh=mesh, in_specs=placed, out_specs=P("expert", "tensor"), check_vma=False)
```

```python
import functools
import math

import jax
import jax.numpy as jnp
from jax import lax
from jax.experimental import pallas as pl
from jax.experimental.pallas import tpu as pltpu
from jax.sharding import PartitionSpec as P

VMEM = pl.BlockSpec(memory_space=pltpu.VMEM)
ANY = pl.BlockSpec(memory_space=pltpu.HBM)
BF16 = jnp.bfloat16
F32 = jnp.float32
FIRST, LAST, CHIP, EARLY = 10, 9, 10, 5


def dot(left, right, dims, precision=None):
    return lax.dot_general(left, right, (dims, ((), ())), precision=precision, preferred_element_type=F32)


def eye(n):
    same = lax.broadcasted_iota(jnp.int32, (n, n), 0) == lax.broadcasted_iota(jnp.int32, (n, n), 1)
    return same.astype(F32).astype(BF16)


def store_turned(ref, value, shift):
    cut = shift % value.shape[0]
    ref[: value.shape[0] - cut] = value[cut:]
    if cut:
        ref[value.shape[0] - cut :] = value[:cut]


def chip_at(i, n):
    return (i + CHIP * n // 16) % n


def call(body, out, operands, flops=0, core=None, far=(), far_out=0, aliases={}, scratch=(), grant=20480):
    scalar = () if core is None else (core,)
    specs = [pl.BlockSpec(memory_space=pltpu.SMEM)] * len(scalar) + [VMEM] * len(operands) + [ANY] * len(far)
    outs = jax.tree.leaves(out)
    moved = sum(math.prod(o.shape) * o.dtype.itemsize for o in (*operands, *outs))
    out_specs = [VMEM] * (len(outs) - far_out) + [ANY] * far_out
    return pl.pallas_call(
        body,
        out_shape=out,
        in_specs=specs,
        out_specs=tuple(out_specs) if isinstance(out, tuple) else out_specs[0],
        input_output_aliases=aliases,
        scratch_shapes=list(scratch),
        compiler_params=pltpu.CompilerParams(vmem_limit_bytes=grant * 2**10),
        cost_estimate=pl.CostEstimate(flops=flops, bytes_accessed=moved, transcendentals=0),
    )(*scalar, *operands, *far)


def fetch(pairs, sems):
    copies = [pltpu.make_async_copy(source, target, sems.at[i]) for i, (source, target) in enumerate(pairs)]
    for copy in copies:
        copy.start()
    return copies


def pick_columns(depth, core, fars, send_far, own_far, weights_ref, send_ref, own_ref, out_sems, sems):
    n = weights_ref.shape[2] // (2 * depth)
    thin = 4 * depth
    stores = []
    for k, load_far in enumerate(fars):
        pltpu.make_async_copy(load_far, weights_ref.at[k], sems.at[k]).wait()
        for which in range(2):

            @pl.when(core == which)
            def _():
                for ref, part in ((send_ref, 1 - which), (own_ref, which)):
                    for g in range(n // 4):
                        starts = [(2 * chip_at(4 * g + i, n) + part) * depth for i in range(4)]
                        pieces = [weights_ref[k, :, start : start + depth] for start in starts]
                        ref[k, :, g * thin : (g + 1) * thin] = jnp.concatenate(pieces, axis=1)

        for i, (ref, far) in enumerate(((send_ref, send_far), (own_ref, own_far))):
            store = pltpu.make_async_copy(ref.at[k], far.at[k], out_sems.at[i, k])
            store.start()
            stores.append(store)
    for store in stores:
        store.wait()


def place_kernel(
    depth, capacity, first, shift, where_ref, tokens_far, routes_far, weight_far, gate_far, up_far, down_far,
    placed_ref, mix_ref, send_far, own_far,
    tokens_ref, routes_ref, weight_ref, weights_ref, send_ref, own_ref, sems, weight_sems, out_sems,
):
    pairs = ((tokens_far, tokens_ref), (routes_far, routes_ref), (weight_far, weight_ref))
    copies = fetch(pairs, sems)
    fars = (gate_far, up_far, down_far)
    early = where_ref[0] < 2 * EARLY

    @pl.when(early)
    def _():
        fetch([(far, weights_ref.at[k]) for k, far in enumerate(fars)], weight_sems)

    for copy in copies:
        copy.wait()
    top, rows = routes_ref.shape
    slots = placed_ref.shape[0]
    slot = lax.broadcasted_iota(jnp.int32, (slots, rows), 0)
    experts = slots // capacity
    expert = (slot // capacity + first) % experts
    spot = slot % capacity
    weight = weight_ref[...].astype(F32)
    share = weight / jnp.sum(weight, axis=0, keepdims=True)
    named = jnp.zeros((slots, rows), F32)
    mix = jnp.zeros((slots, rows), F32)
    for k in range(top):
        hit = routes_ref[k : k + 1, :] == expert
        named += jnp.where(hit, 1.0, 0.0)
        mix += jnp.where(hit, share[k : k + 1, :], 0.0)
    earlier = lax.broadcasted_iota(jnp.int32, (rows, rows), 0) < lax.broadcasted_iota(jnp.int32, (rows, rows), 1)
    before = dot(named.astype(BF16), earlier.astype(F32).astype(BF16), ((1,), (0,)))
    here = (named > 0.5) & (before.astype(jnp.int32) == spot)
    store_turned(mix_ref, jnp.where(here, mix, 0.0), shift)
    dispatch = jnp.where(here, 1.0, 0.0).astype(BF16)
    placed_ref[...] = dot(dispatch, tokens_ref[...], ((1,), (0,))).astype(BF16)

    @pl.when(early)
    def _():
        pick_columns(depth, where_ref[0] % 2, fars, send_far, own_far, weights_ref, send_ref, own_ref, out_sems, weight_sems)


def turn_kernel(arrived_ref, copies_ref):
    n, depth, _ = copies_ref.shape
    turned = dot(eye(depth), arrived_ref[...], ((1,), (1,))).astype(BF16)
    for i in range(n):
        copies_ref[i] = turned


def pick_kernel(
    depth, where_ref, gate_far, up_far, down_far, _, __, send_far, own_far, weights_ref, send_ref, own_ref, sems, out_sems
):
    fars = (gate_far, up_far, down_far)

    @pl.when(where_ref[0] >= 2 * EARLY)
    def _():
        fetch([(far, weights_ref.at[k]) for k, far in enumerate(fars)], sems)
        pick_columns(depth, where_ref[0] % 2, fars, send_far, own_far, weights_ref, send_ref, own_ref, out_sems, sems)


def rise_kernel(core_ref, x_ref, own_ref, got_ref, out_ref):
    n, depth, slots = x_ref.shape
    x = x_ref[...].reshape(n * depth, slots)
    for ref, which in ((own_ref, core_ref[0]), (got_ref, 1 - core_ref[0])):
        for k in range(2):
            out_ref[2 * which + k] = dot(ref[k], x, ((1,), (0,))).astype(BF16)


def fall_kernel(core_ref, halves_ref, own_ref, got_ref, out_ref):
    n, depth, _ = out_ref.shape
    hidden = []
    for u in (core_ref[0], 1 - core_ref[0]):
        gate = halves_ref[2 * u].astype(F32) + halves_ref[4 + 2 * u].astype(F32)
        up = halves_ref[2 * u + 1].astype(F32) + halves_ref[5 + 2 * u].astype(F32)
        hidden.append((gate / (1.0 + jnp.exp(-gate)) * up).astype(BF16))
    group = 4
    for g in range(n // group):
        columns = slice(g * group * depth, (g + 1) * group * depth)
        part = dot(own_ref[2, :, columns], hidden[0], ((0,), (0,)))
        part += dot(got_ref[2, :, columns], hidden[1], ((0,), (0,)))
        for j in range(group):
            out_ref[g * group + j] = part[j * depth : (j + 1) * depth].astype(BF16)


def sum_kernel(shift, pieces_ref, out_ref):
    n, depth, _ = pieces_ref.shape
    total = pieces_ref[0].astype(F32)
    for i in range(1, n):
        total += pieces_ref[i].astype(F32)
    store_turned(out_ref, dot(total.astype(BF16), eye(depth), ((0,), (0,))).astype(BF16), shift)


def mix_kernel(mix_ref, returned_ref, out_ref):
    rest = mix_ref[...]
    values = returned_ref[...]
    total = jnp.zeros(out_ref.shape, F32)
    for _ in range(3):
        piece = rest.astype(BF16)
        rest = rest - piece.astype(F32)
        total += dot(piece, values, ((0,), (0,)))
    out_ref[...] = total.astype(BF16)


def local(tokens, routes, route_weight, w_gate, w_up, w_down):
    experts, chips = lax.axis_size("expert"), lax.axis_size("tensor") // 2
    rows, depth = tokens.shape
    units, width = w_gate.shape[1:]
    half = width // 2
    padded = -(-units // 16) * 16
    capacity = min(rows, 2 * rows * routes.shape[1] // experts)
    slots = experts * capacity
    first, last = FIRST * experts // 16, LAST * experts // 16
    order_out = [[(i + first) % experts for i in range(experts)]]
    order_back = [[(i + last) % experts for i in range(experts)]]
    shift = (last - first) * capacity
    same_core = [[2 * chip_at(i, chips) + c for i in range(chips)] for c in range(2)]
    same_chip = [[2 * i, 2 * i + 1] for i in range(chips)]
    core = (lax.axis_index("tensor") % 2).astype(jnp.int32).reshape(1)
    where = (lax.axis_index("expert") * 2 + lax.axis_index("tensor") % 2).astype(jnp.int32).reshape(1)

    def shape(*dims, dtype=BF16):
        return jax.ShapeDtypeStruct(dims, dtype)

    weights = (w_gate[0], w_up[0], w_down[0])
    thirds = shape(3, units, half)
    picking = (
        pltpu.VMEM((3, units, width), BF16),
        pltpu.VMEM(thirds.shape, BF16),
        pltpu.VMEM(thirds.shape, BF16),
    )
    placed, mix, send, own = call(
        functools.partial(place_kernel, depth, capacity, first, shift),
        (shape(slots, depth), shape(slots, rows, dtype=F32), thirds, thirds),
        (),
        core=where,
        far=(tokens, routes.T, route_weight.T, *weights),
        far_out=2,
        scratch=(
            pltpu.VMEM(tokens.shape, tokens.dtype),
            pltpu.VMEM(routes.shape[::-1], routes.dtype),
            pltpu.VMEM(routes.shape[::-1], route_weight.dtype),
            *picking,
            *[pltpu.SemaphoreType.DMA((3,))] * 2,
            pltpu.SemaphoreType.DMA((2, 3)),
        ),
        grant=65536,
    )
    arrived = lax.all_to_all(placed.reshape(experts, capacity, depth), "expert", 0, 0, axis_index_groups=order_out, tiled=True)

    send, own = call(
        functools.partial(pick_kernel, depth),
        (thirds, thirds),
        (),
        flops=10**8,
        core=where,
        far=(*weights, send, own),
        far_out=2,
        aliases={4: 0, 5: 1},
        scratch=(*picking, pltpu.SemaphoreType.DMA((3,)), pltpu.SemaphoreType.DMA((2, 3))),
        grant=65024,
    )
    got = lax.ppermute(send, "tensor", [(i, i ^ 1) for i in range(2 * chips)])
    copies = call(turn_kernel, shape(chips, depth, slots), (arrived.reshape(slots, depth),), flops=10**11)
    x = lax.all_to_all(copies, "tensor", 0, 0, axis_index_groups=same_core, tiled=True)
    partial = call(
        rise_kernel,
        shape(4, units, slots),
        (x, own, got),
        flops=2 * 4 * units * half * slots,
        core=core,
    )
    halves = lax.all_gather(partial, "tensor", axis=0, axis_index_groups=same_chip, tiled=True)
    part = call(
        fall_kernel,
        shape(chips, depth, slots),
        (halves, own, got),
        flops=2 * 2 * units * half * slots,
        core=core,
    )
    pieces = lax.all_to_all(part, "tensor", 0, 0, axis_index_groups=same_core, tiled=True)
    summed = call(functools.partial(sum_kernel, shift), shape(slots, depth), (pieces,))
    returned = lax.all_to_all(summed.reshape(experts, capacity, depth), "expert", 0, 0, axis_index_groups=order_back, tiled=True)
    return call(mix_kernel, shape(rows, depth), (mix, returned.reshape(slots, depth)))


def solution(mesh):
    placed = (
        P("expert", "tensor"),
        P("expert", None),
        P("expert", None),
        P("expert", "tensor", None),
        P("expert", "tensor", None),
        P("expert", "tensor", None),
    )
    return jax.shard_map(local, mesh=mesh, in_specs=placed, out_specs=P("expert", "tensor"), check_vma=False)
```

```python
import functools
import math

import jax
import jax.numpy as jnp
from jax import lax
from jax.experimental import pallas as pl
from jax.experimental.pallas import tpu as pltpu
from jax.sharding import PartitionSpec as P

VMEM = pl.BlockSpec(memory_space=pltpu.VMEM)
ANY = pl.BlockSpec(memory_space=pltpu.HBM)
BF16 = jnp.bfloat16
F32 = jnp.float32
FIRST, LAST, CHIP, EARLY = 10, 9, 10, 4


def dot(left, right, dims, precision=None):
    return lax.dot_general(left, right, (dims, ((), ())), precision=precision, preferred_element_type=F32)


def eye(n):
    same = lax.broadcasted_iota(jnp.int32, (n, n), 0) == lax.broadcasted_iota(jnp.int32, (n, n), 1)
    return same.astype(F32).astype(BF16)


def store_turned(ref, value, shift):
    cut = shift % value.shape[0]
    ref[: value.shape[0] - cut] = value[cut:]
    if cut:
        ref[value.shape[0] - cut :] = value[:cut]


def chip_at(i, n):
    return (i + CHIP * n // 16) % n


def call(body, out, operands, flops=0, core=None, far=(), far_out=0, aliases={}, scratch=(), grant=20480):
    scalar = () if core is None else (core,)
    specs = [pl.BlockSpec(memory_space=pltpu.SMEM)] * len(scalar) + [VMEM] * len(operands) + [ANY] * len(far)
    outs = jax.tree.leaves(out)
    moved = sum(math.prod(o.shape) * o.dtype.itemsize for o in (*operands, *outs))
    out_specs = [VMEM] * (len(outs) - far_out) + [ANY] * far_out
    return pl.pallas_call(
        body,
        out_shape=out,
        in_specs=specs,
        out_specs=tuple(out_specs) if isinstance(out, tuple) else out_specs[0],
        input_output_aliases=aliases,
        scratch_shapes=list(scratch),
        compiler_params=pltpu.CompilerParams(vmem_limit_bytes=grant * 2**10),
        cost_estimate=pl.CostEstimate(flops=flops, bytes_accessed=moved, transcendentals=0),
    )(*scalar, *operands, *far)


def fetch(pairs, sems):
    copies = [pltpu.make_async_copy(source, target, sems.at[i]) for i, (source, target) in enumerate(pairs)]
    for copy in copies:
        copy.start()
    return copies


def pick_columns(depth, core, fars, send_far, own_far, weights_ref, send_ref, own_ref, out_sems, sems):
    n = weights_ref.shape[2] // (2 * depth)
    thin = 4 * depth
    stores = []
    for k, load_far in enumerate(fars):
        pltpu.make_async_copy(load_far, weights_ref.at[k], sems.at[k]).wait()
        for which in range(2):

            @pl.when(core == which)
            def _():
                for ref, part in ((send_ref, 1 - which), (own_ref, which)):
                    for g in range(n // 4):
                        starts = [(2 * chip_at(4 * g + i, n) + part) * depth for i in range(4)]
                        pieces = [weights_ref[k, :, start : start + depth] for start in starts]
                        ref[k, :, g * thin : (g + 1) * thin] = jnp.concatenate(pieces, axis=1)

        for i, (ref, far) in enumerate(((send_ref, send_far), (own_ref, own_far))):
            store = pltpu.make_async_copy(ref.at[k], far.at[k], out_sems.at[i, k])
            store.start()
            stores.append(store)
    for store in stores:
        store.wait()


def place_kernel(
    depth, capacity, first, shift, where_ref, tokens_far, routes_far, weight_far, gate_far, up_far, down_far,
    placed_ref, mix_ref, send_far, own_far,
    tokens_ref, routes_ref, weight_ref, weights_ref, send_ref, own_ref, sems, weight_sems, out_sems,
):
    pairs = ((tokens_far, tokens_ref), (routes_far, routes_ref), (weight_far, weight_ref))
    copies = fetch(pairs, sems)
    fars = (gate_far, up_far, down_far)
    early = where_ref[0] < 2 * EARLY

    @pl.when(early)
    def _():
        fetch([(far, weights_ref.at[k]) for k, far in enumerate(fars)], weight_sems)

    for copy in copies:
        copy.wait()
    top, rows = routes_ref.shape
    slots = placed_ref.shape[0]
    slot = lax.broadcasted_iota(jnp.int32, (slots, rows), 0)
    experts = slots // capacity
    expert = (slot // capacity + first) % experts
    spot = slot % capacity
    weight = weight_ref[...].astype(F32)
    share = weight / jnp.sum(weight, axis=0, keepdims=True)
    named = jnp.zeros((slots, rows), F32)
    mix = jnp.zeros((slots, rows), F32)
    for k in range(top):
        hit = routes_ref[k : k + 1, :] == expert
        named += jnp.where(hit, 1.0, 0.0)
        mix += jnp.where(hit, share[k : k + 1, :], 0.0)
    earlier = lax.broadcasted_iota(jnp.int32, (rows, rows), 0) < lax.broadcasted_iota(jnp.int32, (rows, rows), 1)
    before = dot(named.astype(BF16), earlier.astype(F32).astype(BF16), ((1,), (0,)))
    here = (named > 0.5) & (before.astype(jnp.int32) == spot)
    store_turned(mix_ref, jnp.where(here, mix, 0.0), shift)
    dispatch = jnp.where(here, 1.0, 0.0).astype(BF16)
    placed_ref[...] = dot(dispatch, tokens_ref[...], ((1,), (0,))).astype(BF16)

    @pl.when(early)
    def _():
        pick_columns(depth, where_ref[0] % 2, fars, send_far, own_far, weights_ref, send_ref, own_ref, out_sems, weight_sems)


def turn_kernel(arrived_ref, copies_ref):
    n, depth, _ = copies_ref.shape
    turned = dot(eye(depth), arrived_ref[...], ((1,), (1,))).astype(BF16)
    for i in range(n):
        copies_ref[i] = turned


def pick_kernel(
    depth, where_ref, gate_far, up_far, down_far, _, __, send_far, own_far, weights_ref, send_ref, own_ref, sems, out_sems
):
    fars = (gate_far, up_far, down_far)

    @pl.when(where_ref[0] >= 2 * EARLY)
    def _():
        fetch([(far, weights_ref.at[k]) for k, far in enumerate(fars)], sems)
        pick_columns(depth, where_ref[0] % 2, fars, send_far, own_far, weights_ref, send_ref, own_ref, out_sems, sems)


def rise_kernel(core_ref, x_ref, own_ref, got_ref, out_ref):
    n, depth, slots = x_ref.shape
    x = x_ref[...].reshape(n * depth, slots)
    for ref, which in ((own_ref, core_ref[0]), (got_ref, 1 - core_ref[0])):
        for k in range(2):
            out_ref[2 * which + k] = dot(ref[k], x, ((1,), (0,))).astype(BF16)


def fall_kernel(core_ref, halves_ref, own_ref, got_ref, out_ref):
    n, depth, _ = out_ref.shape
    hidden = []
    for u in (core_ref[0], 1 - core_ref[0]):
        gate = halves_ref[2 * u].astype(F32) + halves_ref[4 + 2 * u].astype(F32)
        up = halves_ref[2 * u + 1].astype(F32) + halves_ref[5 + 2 * u].astype(F32)
        hidden.append((gate / (1.0 + jnp.exp(-gate)) * up).astype(BF16))
    group = 4
    for g in range(n // group):
        columns = slice(g * group * depth, (g + 1) * group * depth)
        part = dot(own_ref[2, :, columns], hidden[0], ((0,), (0,)))
        part += dot(got_ref[2, :, columns], hidden[1], ((0,), (0,)))
        for j in range(group):
            out_ref[g * group + j] = part[j * depth : (j + 1) * depth].astype(BF16)


def sum_kernel(shift, pieces_ref, out_ref):
    n, depth, _ = pieces_ref.shape
    total = pieces_ref[0].astype(F32)
    for i in range(1, n):
        total += pieces_ref[i].astype(F32)
    store_turned(out_ref, dot(total.astype(BF16), eye(depth), ((0,), (0,))).astype(BF16), shift)


def mix_kernel(mix_ref, returned_ref, out_ref):
    rest = mix_ref[...]
    values = returned_ref[...]
    total = jnp.zeros(out_ref.shape, F32)
    for _ in range(3):
        piece = rest.astype(BF16)
        rest = rest - piece.astype(F32)
        total += dot(piece, values, ((0,), (0,)))
    out_ref[...] = total.astype(BF16)


def local(tokens, routes, route_weight, w_gate, w_up, w_down):
    experts, chips = lax.axis_size("expert"), lax.axis_size("tensor") // 2
    rows, depth = tokens.shape
    units, width = w_gate.shape[1:]
    half = width // 2
    padded = -(-units // 16) * 16
    capacity = min(rows, 2 * rows * routes.shape[1] // experts)
    slots = experts * capacity
    first, last = FIRST * experts // 16, LAST * experts // 16
    order_out = [[(i + first) % experts for i in range(experts)]]
    order_back = [[(i + last) % experts for i in range(experts)]]
    shift = (last - first) * capacity
    same_core = [[2 * chip_at(i, chips) + c for i in range(chips)] for c in range(2)]
    same_chip = [[2 * i, 2 * i + 1] for i in range(chips)]
    core = (lax.axis_index("tensor") % 2).astype(jnp.int32).reshape(1)
    where = (lax.axis_index("expert") * 2 + lax.axis_index("tensor") % 2).astype(jnp.int32).reshape(1)

    def shape(*dims, dtype=BF16):
        return jax.ShapeDtypeStruct(dims, dtype)

    weights = (w_gate[0], w_up[0], w_down[0])
    thirds = shape(3, units, half)
    picking = (
        pltpu.VMEM((3, units, width), BF16),
        pltpu.VMEM(thirds.shape, BF16),
        pltpu.VMEM(thirds.shape, BF16),
    )
    placed, mix, send, own = call(
        functools.partial(place_kernel, depth, capacity, first, shift),
        (shape(slots, depth), shape(slots, rows, dtype=F32), thirds, thirds),
        (),
        core=where,
        far=(tokens, routes.T, route_weight.T, *weights),
        far_out=2,
        scratch=(
            pltpu.VMEM(tokens.shape, tokens.dtype),
            pltpu.VMEM(routes.shape[::-1], routes.dtype),
            pltpu.VMEM(routes.shape[::-1], route_weight.dtype),
            *picking,
            *[pltpu.SemaphoreType.DMA((3,))] * 2,
            pltpu.SemaphoreType.DMA((2, 3)),
        ),
        grant=65536,
    )
    arrived = lax.all_to_all(placed.reshape(experts, capacity, depth), "expert", 0, 0, axis_index_groups=order_out, tiled=True)

    send, own = call(
        functools.partial(pick_kernel, depth),
        (thirds, thirds),
        (),
        flops=10**8,
        core=where,
        far=(*weights, send, own),
        far_out=2,
        aliases={4: 0, 5: 1},
        scratch=(*picking, pltpu.SemaphoreType.DMA((3,)), pltpu.SemaphoreType.DMA((2, 3))),
        grant=65024,
    )
    got = lax.ppermute(send, "tensor", [(i, i ^ 1) for i in range(2 * chips)])
    copies = call(turn_kernel, shape(chips, depth, slots), (arrived.reshape(slots, depth),), flops=10**11)
    x = lax.all_to_all(copies, "tensor", 0, 0, axis_index_groups=same_core, tiled=True)
    partial = call(
        rise_kernel,
        shape(4, units, slots),
        (x, own, got),
        flops=2 * 4 * units * half * slots,
        core=core,
    )
    halves = lax.all_gather(partial, "tensor", axis=0, axis_index_groups=same_chip, tiled=True)
    part = call(
        fall_kernel,
        shape(chips, depth, slots),
        (halves, own, got),
        flops=2 * 2 * units * half * slots,
        core=core,
    )
    pieces = lax.all_to_all(part, "tensor", 0, 0, axis_index_groups=same_core, tiled=True)
    summed = call(functools.partial(sum_kernel, shift), shape(slots, depth), (pieces,))
    returned = lax.all_to_all(summed.reshape(experts, capacity, depth), "expert", 0, 0, axis_index_groups=order_back, tiled=True)
    return call(mix_kernel, shape(rows, depth), (mix, returned.reshape(slots, depth)))


def solution(mesh):
    placed = (
        P("expert", "tensor"),
        P("expert", None),
        P("expert", None),
        P("expert", "tensor", None),
        P("expert", "tensor", None),
        P("expert", "tensor", None),
    )
    return jax.shard_map(local, mesh=mesh, in_specs=placed, out_specs=P("expert", "tensor"), check_vma=False)
```
